256 devices in a mesh: dp: 8 (over x, core), tp: 32 (over y, z).
Axes of the slice: x: 4, y: 4, z: 8, core: 2. Of those that a mesh axis runs over, the one named last changes fastest.
Arguments:
- queries: bfloat16 [2048, 64, 576], P(('dp', 'tp')), may hold values from -40 to 40
- new_key: bfloat16 [2048, 576], P(('dp', 'tp')), may hold values from -8 to 8
- latent_cache: bfloat16 [786432, 576], P(('dp', 'tp')), may hold values from -8 to 8
- lengths: int32 [2048], P(('dp', 'tp')), may hold values from 1 to 3072, as said below
- counts: int32 [256], P(('dp', 'tp')), may hold values from 1 to 8, as said below
- residual: float32 [2048, 3584], P(('dp', 'tp')), may hold values from -4 to 4
- value_up: bfloat16 [64, 512, 128], P('tp'), may hold values from -0.25 to 0.25
- output_proj: bfloat16 [8192, 3584], P('tp'), may hold values from -0.0625 to 0.0625
- norm_gain: bfloat16 [3584], replicated, may hold values from 0.5 to 2
- gate_up: bfloat16 [2, 3584, 9216], P(None, 'dp', 'tp'), may hold values from -0.09375 to 0.09375
- down_proj: bfloat16 [9216, 3584], P('tp'), may hold values from -0.0625 to 0.0625
Outputs:
- mixed: bfloat16 [2048, 3584], P(('dp', 'tp'))
The draws below stay inside these ranges and needn't reach their ends.
Inputs may be any that keep to these rules, and one draw needn't show every extreme that they name: Slots 0 to counts - 1 of a device are live; in every draw some device has all 8 live. `lengths`: the live slots of one device hold together at most 3072 cached tokens, exactly 3072 on some device of every draw; entries of slots that are not live are stale.
All inputs are finite; a program needn't handle non-finite values.
Results may differ from the reference program's by a relative error of at most 0.014.
Values may be sent and summed in bfloat16 or wider, within the bound.
No kernel may reach another device: no remote copies, remote signals or barrier semaphores. Data moves between devices by JAX's collectives and lax.ppermute only.
A program may use at most 128 MiB of HBM per device.

```python
import math
import jax
import jax.numpy as jnp
from jax import lax

D = 3584
FF = 9216
H = 64
LAT = 512
HEAD_V = 128
SLOTS = 8
POOL = 3072
KDIM = 576
ROWS = 2048
CACHE_ROWS = 786432
DEVICES = 256


def live_layout_drawn(key):
    key = jax.random.fold_in(key, 101)
    key_list = jax.random.split(key, 6)
    device_ids = jnp.arange(DEVICES, dtype=jnp.int32)
    counts = jax.random.randint(key_list[0], (DEVICES,), 1, SLOTS + 1, dtype=jnp.int32)
    full_device = jax.random.randint(key_list[1], (), 0, DEVICES, dtype=jnp.int32)
    counts = jnp.where(device_ids == full_device, SLOTS, counts)
    totals = jax.random.randint(key_list[2], (DEVICES,), POOL // 4, POOL + 1, dtype=jnp.int32)
    offset = jax.random.randint(key_list[3], (), 1, DEVICES, dtype=jnp.int32)
    busy_device = (full_device + offset) % DEVICES
    totals = jnp.where(device_ids == busy_device, POOL, totals)
    counts = jnp.where(device_ids == busy_device, 1, counts)
    slot_ids = jnp.arange(SLOTS, dtype=jnp.int32)[None, :]
    live_mask = slot_ids < counts[:, None]
    shares = jax.random.randint(key_list[4], (DEVICES, SLOTS), 1, 9, dtype=jnp.int32)
    shares = shares * shares * live_mask.astype(jnp.int32)
    extra = totals - counts
    portion = (1 + extra[:, None] * shares // jnp.sum(shares, axis=1, keepdims=True)) * live_mask.astype(jnp.int32)
    portion = portion + jnp.where(slot_ids == 0, (totals - jnp.sum(portion, axis=1))[:, None], 0)
    stale = jax.random.randint(key_list[5], (DEVICES, SLOTS), 1, POOL // SLOTS + 1, dtype=jnp.int32)
    lengths = jnp.where(live_mask, portion, stale)
    return (counts, lengths)


def draw_counts(key, part):
    return live_layout_drawn(key)[0]


def draw_lengths(key, part):
    return live_layout_drawn(key)[1].reshape(ROWS)


def draw_queries(key, part):
    key = jax.random.fold_in(key, 1)
    values = jnp.clip(jax.random.normal(key, (DEVICES, SLOTS, H, KDIM), jnp.float32), -6.0, 6.0)
    return values.reshape(ROWS, H, KDIM).astype(jnp.bfloat16)


def draw_new_key(key, part):
    key = jax.random.fold_in(key, 2)
    values = jnp.clip(jax.random.normal(key, (DEVICES, SLOTS, KDIM), jnp.float32), -6.0, 6.0)
    return values.reshape(ROWS, KDIM).astype(jnp.bfloat16)


def draw_latent_cache(key, part):
    key = jax.random.fold_in(key, 3)
    values = jnp.clip(jax.random.normal(key, (DEVICES, POOL, KDIM), jnp.float32), -6.0, 6.0)
    return values.reshape(CACHE_ROWS, KDIM).astype(jnp.bfloat16)


def level_of(own_key, shape, cuts, low, high):
    level = 1.0
    for axis_at, shards_of in cuts:
        heights = jax.random.uniform(jax.random.fold_in(jax.random.fold_in(own_key, 6), axis_at), (shards_of,), jnp.float32, low / len(cuts), high / len(cuts))
        level = level * jnp.repeat(jnp.exp(heights), shape[axis_at] // shards_of).reshape((-1,) + (1,) * (len(shape) - 1 - axis_at))
    return level


def noise(own_key, extent, deviation, reach, cuts=(), held_as=jnp.bfloat16):
    gain = level_of(own_key, extent, cuts, -0.22, 0.18) if cuts else 1.0
    values = jax.random.normal(own_key, extent, jnp.float32) * deviation * gain
    return jnp.minimum(jnp.maximum(values, -reach), reach).astype(held_as)


def setup_inputs(seed: int = 0) -> dict:
    streams_of = jax.random.split(jax.random.key(seed), 12)
    queries = draw_queries(jax.random.fold_in(streams_of[11], 71), 0)
    new_key = draw_new_key(jax.random.fold_in(streams_of[11], 71), 0)
    latent_cache = draw_latent_cache(jax.random.fold_in(streams_of[11], 71), 0)
    lengths = draw_lengths(jax.random.fold_in(streams_of[11], 71), 0)
    counts = draw_counts(jax.random.fold_in(streams_of[11], 71), 0)
    residual = noise(streams_of[5], (ROWS, D), 0.5, 4.0, ((0, 256),), jnp.float32)
    value_up = noise(streams_of[6], (H, LAT, HEAD_V), LAT ** -0.5, 0.25, ((0, 32),))
    output_proj = noise(streams_of[7], (H * HEAD_V, D), (H * HEAD_V) ** -0.5, 0.0625, ((0, 32),))
    norm_gain = jnp.clip(jnp.exp(jax.random.uniform(streams_of[8], (D,), jnp.float32, math.log(0.5), math.log(2.0))), 0.5, 2.0).astype(jnp.bfloat16)
    gate_up = noise(streams_of[9], (2, D, FF), D ** -0.5, 0.09375, ((1, 8), (2, 32)))
    down_proj = noise(streams_of[10], (FF, D), FF ** -0.5, 0.0625, ((0, 32),))
    return {"queries": queries, "new_key": new_key, "latent_cache": latent_cache, "lengths": lengths, "counts": counts, "residual": residual, "value_up": value_up, "output_proj": output_proj, "norm_gain": norm_gain, "gate_up": gate_up, "down_proj": down_proj}


SOFTMAX_SCALE = 192.0 ** (-0.5)
NORM_EPS = 1e-06

def live_layout(lengths, counts):
    length_grid = lengths.reshape(DEVICES, SLOTS)
    slot_ids = jnp.arange(SLOTS, dtype=jnp.int32)
    live_mask = slot_ids[None, :] < counts[:, None]
    used_lengths = jnp.where(live_mask, length_grid, jnp.zeros_like(length_grid))
    start_rows = jnp.cumsum(used_lengths, axis=1).astype(jnp.int32) - used_lengths
    return (live_mask, used_lengths, start_rows)

def attend_device(pieces):
    query_part, new_part, pool_part, used_part, start_part = pieces
    query_float = query_part.astype(jnp.float32)
    pool_float = pool_part.astype(jnp.float32)
    new_float = new_part.astype(jnp.float32)
    scores = jnp.einsum('shk,tk->sht', query_float, pool_float, precision=lax.Precision.HIGHEST) * SOFTMAX_SCALE
    positions = jnp.arange(POOL, dtype=jnp.int32)
    inside = (positions[None, :] >= start_part[:, None]) & (positions[None, :] < (start_part + used_part)[:, None])
    scores = jnp.where(inside[:, None, :], scores, -jnp.inf)
    own_score = jnp.einsum('shk,sk->sh', query_float, new_float, precision=lax.Precision.HIGHEST) * SOFTMAX_SCALE
    top_score = jnp.maximum(lax.optimization_barrier(jnp.max(scores, axis=-1)), own_score)
    probs = jnp.where(inside[:, None, :], jnp.exp(scores - top_score[..., None]), 0.0)
    own_prob = jnp.exp(own_score - top_score)
    denominator = lax.optimization_barrier(jnp.sum(probs, axis=-1)) + own_prob
    probs_round = lax.optimization_barrier(probs.astype(jnp.bfloat16)).astype(jnp.float32)
    own_round = lax.optimization_barrier(own_prob.astype(jnp.bfloat16)).astype(jnp.float32)
    summed = jnp.einsum('sht,tc->shc', probs_round, pool_float[:, :LAT], precision=lax.Precision.HIGHEST)
    summed = summed + own_round[..., None] * new_float[:, None, :LAT]
    return (summed / denominator[..., None]).astype(jnp.bfloat16)

def reference(queries, new_key, latent_cache, lengths, counts, residual, value_up, output_proj, norm_gain, gate_up, down_proj):
    live_mask, used_lengths, start_rows = live_layout(lengths, counts)
    latent_out = lax.map(attend_device, (queries.reshape(DEVICES, SLOTS, H, KDIM), new_key.reshape(DEVICES, SLOTS, KDIM), latent_cache.reshape(DEVICES, POOL, KDIM), used_lengths, start_rows))
    latent_out = latent_out.reshape(ROWS, H, LAT)
    values = jnp.einsum('rhc,hcj->rhj', latent_out.astype(jnp.float32), value_up.astype(jnp.float32), precision=lax.Precision.HIGHEST)
    values = values.astype(jnp.bfloat16).reshape(ROWS, H * HEAD_V)
    state = residual + jnp.dot(values, output_proj, preferred_element_type=jnp.float32)
    mean_square = lax.optimization_barrier(jnp.mean(state * state, axis=-1, keepdims=True))
    normed = (state * lax.rsqrt(mean_square + NORM_EPS) * norm_gain.astype(jnp.float32)).astype(jnp.bfloat16)
    gate = jnp.dot(normed, gate_up[0], preferred_element_type=jnp.float32)
    upward = jnp.dot(normed, gate_up[1], preferred_element_type=jnp.float32)
    hidden = (jax.nn.silu(gate) * upward).astype(jnp.bfloat16)
    mixed = state + jnp.dot(hidden, down_proj, preferred_element_type=jnp.float32)
    return jnp.where(live_mask.reshape(ROWS)[:, None], mixed, 0.0).astype(jnp.bfloat16)
```

```python
import functools

import jax
import jax.numpy as jnp
from jax import lax
from jax.experimental import pallas as pl
from jax.experimental.pallas import tpu as pltpu
from jax.sharding import PartitionSpec as P

SOFTMAX_SCALE = 192.0 ** (-0.5)
NORM_EPS = 1e-06
Y_SIZE = 4
Z_SIZE = 8
BLOCK = 512
Z_GROUPS = [[y * Z_SIZE + z for z in range(Z_SIZE)] for y in range(Y_SIZE)]
BF16 = jnp.bfloat16
F32 = jnp.float32
VMEM = pl.BlockSpec(memory_space=pltpu.VMEM)
SMEM = pl.BlockSpec(memory_space=pltpu.SMEM)
PARAMS = pltpu.CompilerParams(vmem_limit_bytes=40 * 1024 * 1024)


def y_shift(array, step):
    pairs = [
        (y * Z_SIZE + z, ((y + step) % Y_SIZE) * Z_SIZE + z)
        for y in range(Y_SIZE)
        for z in range(Z_SIZE)
    ]
    return lax.ppermute(array, "tp", pairs)


def z_exchange(array):
    return lax.all_to_all(
        array, "tp", split_axis=0, concat_axis=0, tiled=True, axis_index_groups=Z_GROUPS
    )


def attend_kernel(bounds_ref, query_ref, new_key_ref, keys_ref, out_ref, acc_ref):
    slots, heads = 8, 64
    latent = out_ref.shape[1]
    for pair in range(slots // 2):
        first = 2 * pair
        rows = pl.ds(first * heads, 2 * heads)
        query = query_ref[rows, :]
        own_rows = []
        for s in (first, first + 1):
            own_rows.append(
                jnp.broadcast_to(new_key_ref[s : s + 1, :].astype(F32), (heads, query.shape[1]))
            )
        own_keys = jnp.concatenate(own_rows, axis=0)
        own_score = (
            jnp.sum(query.astype(F32) * own_keys, axis=1, keepdims=True) * SOFTMAX_SCALE
        )
        acc_ref[...] = own_keys[:, :latent]
        is_second = lax.broadcasted_iota(jnp.int32, (2 * heads, 1), 0) >= heads
        row_start = jnp.where(is_second, bounds_ref[first + 1], bounds_ref[first])
        row_end = jnp.where(is_second, bounds_ref[first + 2], bounds_ref[first + 1])
        begin = bounds_ref[first] // BLOCK
        end = (bounds_ref[first + 2] + BLOCK - 1) // BLOCK

        def step(block, carry):
            top, total = carry
            offset = pl.multiple_of(block * BLOCK, BLOCK)
            scores = (
                jnp.dot(query, keys_ref[:, pl.ds(offset, BLOCK)], preferred_element_type=F32)
                * SOFTMAX_SCALE
            )
            positions = offset + lax.broadcasted_iota(jnp.int32, (1, BLOCK), 1)
            inside = (positions >= row_start) & (positions < row_end)
            scores = jnp.where(inside, scores, -1e30)
            new_top = jnp.maximum(top, jnp.max(scores, axis=1, keepdims=True))
            decay = jnp.exp(top - new_top)
            probs = jnp.exp(scores - new_top)
            new_total = total * decay + jnp.sum(probs, axis=1, keepdims=True)
            acc_ref[...] = acc_ref[...] * decay + lax.dot_general(
                probs.astype(BF16),
                keys_ref[:latent, pl.ds(offset, BLOCK)],
                (((1,), (1,)), ((), ())),
                preferred_element_type=F32,
            )
            return new_top, new_total

        _, total = lax.fori_loop(begin, end, step, (own_score, jnp.ones_like(own_score)))
        out_ref[rows, :] = (acc_ref[...] / total).astype(BF16)


def attend(bounds, queries, new_key, keys_t, latent):
    slots, heads, width = queries.shape
    rows = slots * heads
    return pl.pallas_call(
        attend_kernel,
        out_shape=jax.ShapeDtypeStruct((rows, latent), BF16),
        in_specs=[SMEM, VMEM, VMEM, VMEM],
        out_specs=VMEM,
        scratch_shapes=[pltpu.VMEM((2 * heads, latent), F32)],
        compiler_params=PARAMS,
        name="attend",
    )(bounds, queries.reshape(rows, width), new_key, keys_t)


def project_kernel(y_ref, latent_ref, up_ref, proj_ref, *refs):
    outs, values_ref, turned_ref = refs[:Y_SIZE], refs[Y_SIZE], refs[Y_SIZE + 1]
    head_v = up_ref.shape[2]
    both = jnp.concatenate([up_ref[0], up_ref[1]], axis=1)
    mapped = jnp.dot(latent_ref[...], both, preferred_element_type=F32)
    mapped = mapped.reshape(32, 2, 8, 2 * head_v)
    values_ref[...] = jnp.concatenate(
        [
            mapped[:, 0, :, :head_v].reshape(256, head_v),
            mapped[:, 1, :, head_v:].reshape(256, head_v),
        ],
        axis=1,
    ).astype(BF16)
    for k in range(Y_SIZE):
        source = pl.multiple_of(lax.rem(y_ref[0] + k, Y_SIZE) * 64, 64)
        turned_ref[64 * k : 64 * k + 64, :] = values_ref[pl.ds(source, 64), :]
    width = proj_ref.shape[1]
    for c in range(0, width, 512):
        part = jnp.dot(
            turned_ref[...], proj_ref[:, c : c + 512], preferred_element_type=F32
        ).astype(BF16)
        for k in range(Y_SIZE):
            outs[k][:, c : c + 512] = part[64 * k : 64 * k + 64]


def project(my_y, latent_rows, value_up, output_proj):
    width = output_proj.shape[1]
    return pl.pallas_call(
        project_kernel,
        out_shape=[jax.ShapeDtypeStruct((64, width), BF16)] * Y_SIZE,
        in_specs=[SMEM, VMEM, VMEM, VMEM],
        out_specs=[VMEM] * Y_SIZE,
        scratch_shapes=[pltpu.VMEM((256, 256), BF16), pltpu.VMEM((256, 256), BF16)],
        compiler_params=PARAMS,
        name="project",
    )(my_y, latent_rows, value_up, output_proj)


def feed_kernel(*refs):
    rows_refs = refs[:Y_SIZE]
    gate_ref, down_ref = refs[Y_SIZE], refs[Y_SIZE + 1]
    outs = refs[Y_SIZE + 2 : 2 * Y_SIZE + 2]
    normed_ref, hidden_ref = refs[2 * Y_SIZE + 2 :]
    parts, _, hidden_width, depth = gate_ref.shape
    for k in range(Y_SIZE):
        normed_ref[64 * k : 64 * k + 64, :] = rows_refs[k][...]
    contract = (((1,), (1,)), ((), ()))
    gate = jnp.zeros((256, hidden_width), F32)
    upward = jnp.zeros((256, hidden_width), F32)
    for d in range(parts):
        piece = normed_ref[:, d * depth : (d + 1) * depth]
        gate += lax.dot_general(piece, gate_ref[d, 0], contract, preferred_element_type=F32)
        upward += lax.dot_general(piece, gate_ref[d, 1], contract, preferred_element_type=F32)
    hidden_ref[...] = (gate / (1.0 + jnp.exp(-gate)) * upward).astype(BF16)
    width = down_ref.shape[1]
    for c in range(0, width, 512):
        part = jnp.dot(
            hidden_ref[...], down_ref[:, c : c + 512], preferred_element_type=F32
        ).astype(BF16)
        for k in range(Y_SIZE):
            outs[k][:, c : c + 512] = part[64 * k : 64 * k + 64]


def feed(row_blocks, gate_rows, down_proj):
    width = down_proj.shape[1]
    return pl.pallas_call(
        feed_kernel,
        out_shape=[jax.ShapeDtypeStruct((64, width), BF16)] * Y_SIZE,
        in_specs=[VMEM] * (Y_SIZE + 2),
        out_specs=[VMEM] * Y_SIZE,
        scratch_shapes=[
            pltpu.VMEM((256, width), BF16),
            pltpu.VMEM((256, down_proj.shape[0]), BF16),
        ],
        compiler_params=PARAMS,
        name="feed",
    )(*row_blocks, gate_rows, down_proj)


def sum_over_tp(blocks, direction):
    arrived = [blocks[0]] + [y_shift(blocks[k], direction * k) for k in (2, 1, 3)]
    column = sum(block.astype(F32) for block in arrived).astype(BF16)
    pieces = z_exchange(column).reshape(Z_SIZE, 8, column.shape[1])
    return jnp.sum(pieces.astype(F32), axis=0)


def local(
    queries,
    new_key,
    latent_cache,
    lengths,
    counts,
    residual,
    value_up,
    output_proj,
    norm_gain,
    gate_up,
    down_proj,
):
    slots, heads, _ = queries.shape
    latent = value_up.shape[1]
    gate_rows = lax.all_gather(gate_up.transpose(0, 2, 1), "dp", axis=0, tiled=False)

    live_mask = jnp.arange(slots, dtype=jnp.int32) < counts[0]
    used = jnp.where(live_mask, lengths, 0)
    bounds = jnp.concatenate([jnp.zeros((1,), jnp.int32), jnp.cumsum(used)])
    latent_out = attend(bounds, queries, new_key, latent_cache.T, latent)
    outgoing = latent_out.reshape(slots, heads, latent).transpose(1, 0, 2)
    outgoing = outgoing.reshape(32, 2 * slots, latent)
    incoming = lax.all_to_all(outgoing, "tp", split_axis=0, concat_axis=0, tiled=True)

    my_y = (lax.axis_index("tp") // Z_SIZE).astype(jnp.int32).reshape(1)
    terms = project(my_y, incoming.reshape(64 * slots, latent), value_up, output_proj)
    state = sum_over_tp(terms, 1) + residual
    mean_square = jnp.mean(state * state, axis=-1, keepdims=True)
    normed = (state * lax.rsqrt(mean_square + NORM_EPS) * norm_gain.astype(F32)).astype(BF16)

    column = z_exchange(jnp.tile(normed, (Z_SIZE, 1)))
    shifted = {k: y_shift(column, k) for k in (2, 1, 3)}
    blocks = [column] + [shifted[k] for k in (1, 2, 3)]
    terms = feed(blocks, gate_rows, down_proj)
    mixed = sum_over_tp(terms, -1) + state
    return jnp.where(live_mask[:, None], mixed, 0.0).astype(BF16)


def solution(mesh):
    placed = (
        P(("dp", "tp"), None, None),
        P(("dp", "tp"), None),
        P(("dp", "tp"), None),
        P(("dp", "tp")),
        P(("dp", "tp")),
        P(("dp", "tp"), None),
        P("tp", None, None),
        P("tp", None),
        P(),
        P(None, "dp", "tp"),
        P("tp", None),
    )
    return jax.shard_map(
        local, mesh=mesh, in_specs=placed, out_specs=P(("dp", "tp"), None), check_vma=False
    )
```

```python
import functools

import jax
import jax.numpy as jnp
from jax import lax
from jax.experimental import pallas as pl
from jax.experimental.pallas import tpu as pltpu
from jax.sharding import PartitionSpec as P

SOFTMAX_SCALE = 192.0 ** (-0.5)
NORM_EPS = 1e-06
X_SIZE = 4
Y_SIZE = 4
Z_SIZE = 8
BLOCK = 512
Z_GROUPS = [[y * Z_SIZE + z for z in range(Z_SIZE)] for y in range(Y_SIZE)]
BF16 = jnp.bfloat16
F32 = jnp.float32
VMEM = pl.BlockSpec(memory_space=pltpu.VMEM)
SMEM = pl.BlockSpec(memory_space=pltpu.SMEM)
PARAMS = pltpu.CompilerParams(vmem_limit_bytes=40 * 1024 * 1024)


def y_shift(array, step):
    pairs = [
        (y * Z_SIZE + z, ((y + step) % Y_SIZE) * Z_SIZE + z)
        for y in range(Y_SIZE)
        for z in range(Z_SIZE)
    ]
    return lax.ppermute(array, "tp", pairs)


def z_exchange(array):
    return lax.all_to_all(
        array, "tp", split_axis=0, concat_axis=0, tiled=True, axis_index_groups=Z_GROUPS
    )


def block_shapes(width):
    return [jax.ShapeDtypeStruct((rows, width), BF16) for rows in (64, 64, 32, 32, 64)]


def store_blocks(outs, part, column):
    for out, first in zip(outs, (0, 64, 128, 160, 192)):
        rows = out.shape[0]
        out[:, column : column + part.shape[1]] = part[first : first + rows]


def grouped(blocks):
    return [blocks[0], blocks[1], (blocks[2], blocks[3]), blocks[4]]


def dp_shift(array, turn, swap):
    pairs = [
        (2 * x + core, 2 * ((x + turn) % X_SIZE) + (core + swap) % 2)
        for x in range(X_SIZE)
        for core in range(2)
    ]
    return lax.ppermute(array, "dp", pairs)


def attend_kernel(
    bounds_ref,
    all_queries_ref,
    new_key_ref,
    cache_ref,
    out_ref,
    acc_ref,
    query_ref,
    keys_ref,
    seen_ref,
    query_sem,
    sems,
):
    slots, heads = 8, 64
    latent = out_ref.shape[1]
    blocks = (bounds_ref[slots] + BLOCK - 1) // BLOCK

    def arrival(block):
        span = pl.ds(pl.multiple_of(block * BLOCK, BLOCK), BLOCK)
        return pltpu.make_async_copy(cache_ref.at[:, span], keys_ref.at[:, span], sems.at[block])

    query_copy = pltpu.make_async_copy(all_queries_ref, query_ref, query_sem)
    query_copy.start()
    lax.fori_loop(0, blocks, lambda block, _: arrival(block).start(), None)
    seen_ref[0] = 0
    query_copy.wait()
    for pair in range(slots // 2):
        first = 2 * pair
        rows = pl.ds(first * heads, 2 * heads)
        query = query_ref[rows, :]
        own_rows = []
        for s in (first, first + 1):
            own_rows.append(
                jnp.broadcast_to(new_key_ref[s : s + 1, :].astype(F32), (heads, query.shape[1]))
            )
        own_keys = jnp.concatenate(own_rows, axis=0)
        own_score = (
            jnp.sum(query.astype(F32) * own_keys, axis=1, keepdims=True) * SOFTMAX_SCALE
        )
        acc_ref[...] = own_keys[:, :latent]
        is_second = lax.broadcasted_iota(jnp.int32, (2 * heads, 1), 0) >= heads
        row_start = jnp.where(is_second, bounds_ref[first + 1], bounds_ref[first])
        row_end = jnp.where(is_second, bounds_ref[first + 2], bounds_ref[first + 1])
        begin = bounds_ref[first] // BLOCK
        end = (bounds_ref[first + 2] + BLOCK - 1) // BLOCK
        end = jnp.where(bounds_ref[first + 2] > bounds_ref[first], end, begin)

        def step(block, carry):
            top, total = carry

            @pl.when(block == seen_ref[0])
            def _():
                arrival(block).wait()
                seen_ref[0] = block + 1

            offset = pl.multiple_of(block * BLOCK, BLOCK)
            scores = (
                jnp.dot(query, keys_ref[:, pl.ds(offset, BLOCK)], preferred_element_type=F32)
                * SOFTMAX_SCALE
            )
            positions = offset + lax.broadcasted_iota(jnp.int32, (1, BLOCK), 1)
            inside = (positions >= row_start) & (positions < row_end)
            scores = jnp.where(inside, scores, -1e30)
            new_top = jnp.maximum(top, jnp.max(scores, axis=1, keepdims=True))
            decay = jnp.exp(top - new_top)
            probs = jnp.exp(scores - new_top)
            new_total = total * decay + jnp.sum(probs, axis=1, keepdims=True)
            acc_ref[...] = acc_ref[...] * decay + lax.dot_general(
                probs.astype(BF16),
                keys_ref[:latent, pl.ds(offset, BLOCK)],
                (((1,), (1,)), ((), ())),
                preferred_element_type=F32,
            )
            return new_top, new_total

        _, total = lax.fori_loop(begin, end, step, (own_score, jnp.ones_like(own_score)))
        out_ref[rows, :] = (acc_ref[...] / total).astype(BF16)


def attend(bounds, queries, new_key, keys_t, latent):
    slots, heads, width = queries.shape
    rows = slots * heads
    return pl.pallas_call(
        attend_kernel,
        out_shape=jax.ShapeDtypeStruct((rows, latent), BF16),
        in_specs=[
            SMEM,
            pl.BlockSpec(memory_space=pl.ANY),
            VMEM,
            pl.BlockSpec(memory_space=pl.ANY),
        ],
        out_specs=VMEM,
        scratch_shapes=[
            pltpu.VMEM((2 * heads, latent), F32),
            pltpu.VMEM((rows, width), BF16),
            pltpu.VMEM(keys_t.shape, BF16),
            pltpu.SMEM((1,), jnp.int32),
            pltpu.SemaphoreType.DMA,
            pltpu.SemaphoreType.DMA((keys_t.shape[1] // BLOCK,)),
        ],
        compiler_params=pltpu.CompilerParams(vmem_limit_bytes=60 * 1024 * 1024),
        name="attend",
    )(bounds, queries.reshape(rows, width), new_key, keys_t)


def project_kernel(y_ref, latent_ref, up_ref, proj_ref, *refs):
    outs, values_ref, turned_ref = refs[:5], refs[5], refs[6]
    head_v = up_ref.shape[2]
    both = jnp.concatenate([up_ref[0], up_ref[1]], axis=1)
    mapped = jnp.dot(latent_ref[...], both, preferred_element_type=F32)
    mapped = mapped.reshape(32, 2, 8, 2 * head_v)
    values_ref[...] = jnp.concatenate(
        [
            mapped[:, 0, :, :head_v].reshape(256, head_v),
            mapped[:, 1, :, head_v:].reshape(256, head_v),
        ],
        axis=1,
    ).astype(BF16)
    for k in range(Y_SIZE):
        source = pl.multiple_of(lax.rem(y_ref[0] + k, Y_SIZE) * 64, 64)
        turned_ref[64 * k : 64 * k + 64, :] = values_ref[pl.ds(source, 64), :]
    width = proj_ref.shape[1]
    for c in range(0, width, 512):
        part = jnp.dot(
            turned_ref[...], proj_ref[:, c : c + 512], preferred_element_type=F32
        ).astype(BF16)
        store_blocks(outs, part, c)


def project(my_y, latent_rows, value_up, output_proj):
    width = output_proj.shape[1]
    return pl.pallas_call(
        project_kernel,
        out_shape=block_shapes(width),
        in_specs=[SMEM, VMEM, VMEM, VMEM],
        out_specs=[VMEM] * 5,
        scratch_shapes=[pltpu.VMEM((256, 256), BF16), pltpu.VMEM((256, 256), BF16)],
        compiler_params=PARAMS,
        name="project",
    )(my_y, latent_rows, value_up, output_proj)


def feed_kernel(place_ref, *refs):
    rows_refs, gate_refs, down_ref = refs[:5], refs[5:7], refs[7]
    outs, normed_ref, hidden_ref = refs[8:13], refs[13], refs[14]
    _, _, hidden_width, depth = gate_refs[0].shape
    parts = normed_ref.shape[0]
    for rows, first in zip(rows_refs, (0, 64, 128, 160, 192)):
        block = rows[...]
        for d in range(parts):
            normed_ref[d, first : first + rows.shape[0], :] = block[:, d * depth : (d + 1) * depth]
    contract = (((1,), (1,)), ((), ()))
    gate = jnp.zeros((256, hidden_width), F32)
    upward = jnp.zeros((256, hidden_width), F32)
    for k in range(X_SIZE):
        for other in range(2):
            chip = lax.rem(place_ref[1] + X_SIZE - k, X_SIZE)
            core = lax.rem(place_ref[2] + other, 2)
            piece = normed_ref[2 * chip + core]
            gate += lax.dot_general(
                piece, gate_refs[other][k, 0], contract, preferred_element_type=F32
            )
            upward += lax.dot_general(
                piece, gate_refs[other][k, 1], contract, preferred_element_type=F32
            )
    hidden_ref[...] = (gate / (1.0 + jnp.exp(-gate)) * upward).astype(BF16)
    width = down_ref.shape[1]
    for c in range(0, width, 512):
        part = jnp.dot(
            hidden_ref[...], down_ref[:, c : c + 512], preferred_element_type=F32
        ).astype(BF16)
        store_blocks(outs, part, c)


def feed(place, row_blocks, gate_pieces, down_proj):
    width = down_proj.shape[1]
    depth = gate_pieces[0].shape[-1]
    return pl.pallas_call(
        feed_kernel,
        out_shape=block_shapes(width),
        in_specs=[SMEM] + [VMEM] * 8,
        out_specs=[VMEM] * 5,
        scratch_shapes=[
            pltpu.VMEM((width // depth, 256, depth), BF16),
            pltpu.VMEM((256, down_proj.shape[0]), BF16),
        ],
        compiler_params=PARAMS,
        name="feed",
    )(place, *row_blocks, *gate_pieces, down_proj)


def sum_over_y(blocks, direction):
    far = [y_shift(half, 2) for half in blocks[2]]
    near = [y_shift(blocks[k], direction * k) for k in (1, 3)]
    arrived = [blocks[0], jnp.concatenate(far, axis=0)] + near
    return sum(block.astype(F32) for block in arrived).astype(BF16)


def sum_over_z(column):
    pieces = z_exchange(column).reshape(Z_SIZE, 8, column.shape[1])
    return jnp.sum(pieces.astype(F32), axis=0)


def local(
    queries,
    new_key,
    latent_cache,
    lengths,
    counts,
    residual,
    value_up,
    output_proj,
    norm_gain,
    gate_up,
    down_proj,
):
    slots, heads, _ = queries.shape
    latent = value_up.shape[1]
    rank, group = lax.axis_index("tp"), lax.axis_index("dp")
    place = jnp.stack([rank // Z_SIZE, group // 2, group % 2]).astype(jnp.int32)

    live_mask = jnp.arange(slots, dtype=jnp.int32) < counts[0]
    used = jnp.where(live_mask, lengths, 0)
    bounds = jnp.concatenate([jnp.zeros((1,), jnp.int32), jnp.cumsum(used)])
    latent_out = attend(bounds, queries, new_key, latent_cache.T, latent)
    outgoing = latent_out.reshape(slots, heads, latent).transpose(1, 0, 2)
    outgoing = outgoing.reshape(32, 2 * slots, latent)
    incoming = lax.all_to_all(outgoing, "tp", split_axis=0, concat_axis=0, tiled=True)
    gate_own = gate_up.transpose(0, 2, 1)
    gate_pieces = [gate_own] + [dp_shift(gate_own, k, 0) for k in (1, 2, 3)]
    incoming, gate_pieces[1], gate_pieces[3] = lax.optimization_barrier(
        (incoming, gate_pieces[1], gate_pieces[3])
    )

    terms = project(place, incoming.reshape(64 * slots, latent), value_up, output_proj)
    column = sum_over_y(grouped(terms), 1)
    column, gate_pieces[2] = lax.optimization_barrier((column, gate_pieces[2]))
    gate_mine = jnp.stack(gate_pieces)
    gate_mine = [gate_mine, dp_shift(gate_mine, 0, 1)]
    state = sum_over_z(column) + residual
    mean_square = jnp.mean(state * state, axis=-1, keepdims=True)
    normed = (state * lax.rsqrt(mean_square + NORM_EPS) * norm_gain.astype(F32)).astype(BF16)

    column = z_exchange(jnp.tile(normed, (Z_SIZE, 1)))
    far = [y_shift(column[first : first + 32], 2) for first in (0, 32)]
    blocks = [column, y_shift(column, 1), *far, y_shift(column, 3)]
    terms = feed(place, blocks, gate_mine, down_proj)
    mixed = sum_over_z(sum_over_y(grouped(terms), -1)) + state
    return jnp.where(live_mask[:, None], mixed, 0.0).astype(BF16)


def solution(mesh):
    placed = (
        P(("dp", "tp"), None, None),
        P(("dp", "tp"), None),
        P(("dp", "tp"), None),
        P(("dp", "tp")),
        P(("dp", "tp")),
        P(("dp", "tp"), None),
        P("tp", None, None),
        P("tp", None),
        P(),
        P(None, "dp", "tp"),
        P("tp", None),
    )
    return jax.shard_map(
        local, mesh=mesh, in_specs=placed, out_specs=P(("dp", "tp"), None), check_vma=False
    )
```

```python
import functools

import jax
import jax.numpy as jnp
from jax import lax
from jax.experimental import pallas as pl
from jax.experimental.pallas import tpu as pltpu
from jax.sharding import PartitionSpec as P

SOFTMAX_SCALE = 192.0 ** (-0.5)
NORM_EPS = 1e-06
X_SIZE = 4
Y_SIZE = 4
Z_SIZE = 8
BLOCK = 512
Z_GROUPS = [[y * Z_SIZE + z for z in range(Z_SIZE)] for y in range(Y_SIZE)]
BF16 = jnp.bfloat16
F32 = jnp.float32
VMEM = pl.BlockSpec(memory_space=pltpu.VMEM)
SMEM = pl.BlockSpec(memory_space=pltpu.SMEM)
PARAMS = pltpu.CompilerParams(vmem_limit_bytes=40 * 1024 * 1024)


def y_shift(array, step):
    pairs = [
        (y * Z_SIZE + z, ((y + step) % Y_SIZE) * Z_SIZE + z)
        for y in range(Y_SIZE)
        for z in range(Z_SIZE)
    ]
    return lax.ppermute(array, "tp", pairs)


def z_exchange(array):
    return lax.all_to_all(
        array, "tp", split_axis=0, concat_axis=0, tiled=True, axis_index_groups=Z_GROUPS
    )


def block_shapes(width):
    return [jax.ShapeDtypeStruct((rows, width), BF16) for rows in (64, 64, 32, 32, 64)]


def store_blocks(outs, part, column):
    for out, first in zip(outs, (0, 64, 128, 160, 192)):
        rows = out.shape[0]
        out[:, column : column + part.shape[1]] = part[first : first + rows]


def grouped(blocks):
    return [blocks[0], blocks[1], (blocks[2], blocks[3]), blocks[4]]


def dp_shift(array, turn, swap):
    pairs = [
        (2 * x + core, 2 * ((x + turn) % X_SIZE) + (core + swap) % 2)
        for x in range(X_SIZE)
        for core in range(2)
    ]
    return lax.ppermute(array, "dp", pairs)


def attend_kernel(
    lengths_ref,
    counts_ref,
    all_queries_ref,
    new_key_ref,
    cache_ref,
    out_ref,
    acc_ref,
    turned_ref,
    query_ref,
    keys_ref,
    bounds_ref,
    seen_ref,
    query_sem,
    sems,
):
    slots, heads = 8, 64
    latent = out_ref.shape[1]
    query_copy = pltpu.make_async_copy(all_queries_ref, query_ref, query_sem)
    query_copy.start()
    bounds_ref[0] = 0
    for s in range(slots):
        bounds_ref[s + 1] = bounds_ref[s] + jnp.where(s < counts_ref[0], lengths_ref[s], 0)
    blocks = (bounds_ref[slots] + BLOCK - 1) // BLOCK

    def arrival(block):
        span = pl.ds(pl.multiple_of(block * BLOCK, BLOCK), BLOCK)
        return pltpu.make_async_copy(cache_ref.at[:, span], keys_ref.at[:, span], sems.at[block])

    lax.fori_loop(0, blocks, lambda block, _: arrival(block).start(), None)
    seen_ref[0] = 0
    query_copy.wait()
    for pair in range(slots // 2):
        first = 2 * pair
        rows = pl.ds(first * heads, 2 * heads)
        query = query_ref[rows, :]
        own_rows = []
        for s in (first, first + 1):
            own_rows.append(
                jnp.broadcast_to(new_key_ref[s : s + 1, :].astype(F32), (heads, query.shape[1]))
            )
        own_keys = jnp.concatenate(own_rows, axis=0)
        own_score = (
            jnp.sum(query.astype(F32) * own_keys, axis=1, keepdims=True) * SOFTMAX_SCALE
        )
        acc_ref[...] = own_keys[:, :latent]
        is_second = lax.broadcasted_iota(jnp.int32, (2 * heads, 1), 0) >= heads
        row_start = jnp.where(is_second, bounds_ref[first + 1], bounds_ref[first])
        row_end = jnp.where(is_second, bounds_ref[first + 2], bounds_ref[first + 1])
        begin = bounds_ref[first] // BLOCK
        end = (bounds_ref[first + 2] + BLOCK - 1) // BLOCK
        end = jnp.where(bounds_ref[first + 2] > bounds_ref[first], end, begin)

        def step(block, carry):
            top, total = carry

            @pl.when(block == seen_ref[0])
            def _():
                arrival(block).wait()
                seen_ref[0] = block + 1

            offset = pl.multiple_of(block * BLOCK, BLOCK)
            scores = (
                jnp.dot(query, keys_ref[:, pl.ds(offset, BLOCK)], preferred_element_type=F32)
                * SOFTMAX_SCALE
            )
            positions = offset + lax.broadcasted_iota(jnp.int32, (1, BLOCK), 1)
            inside = (positions >= row_start) & (positions < row_end)
            scores = jnp.where(inside, scores, -1e30)
            new_top = jnp.maximum(top, jnp.max(scores, axis=1, keepdims=True))
            decay = jnp.exp(top - new_top)
            probs = jnp.exp(scores - new_top)
            new_total = total * decay + jnp.sum(probs, axis=1, keepdims=True)
            acc_ref[...] = acc_ref[...] * decay + lax.dot_general(
                probs.astype(BF16),
                keys_ref[:latent, pl.ds(offset, BLOCK)],
                (((1,), (1,)), ((), ())),
                preferred_element_type=F32,
            )
            return new_top, new_total

        _, total = lax.fori_loop(begin, end, step, (own_score, jnp.ones_like(own_score)))
        result = acc_ref[...] / total
        for s in (0, 1):
            for c in range(latent // 128):
                turned_ref[c, pl.ds(first + s, heads, slots), :] = result[
                    s * heads : (s + 1) * heads, 128 * c : 128 * c + 128
                ]
    for c in range(latent // 128):
        out_ref[:, 128 * c : 128 * c + 128] = turned_ref[c].astype(BF16)


def attend(lengths, counts, queries, new_key, keys_t, latent):
    slots, heads, width = queries.shape
    rows = slots * heads
    return pl.pallas_call(
        attend_kernel,
        out_shape=jax.ShapeDtypeStruct((rows, latent), BF16),
        in_specs=[
            SMEM,
            SMEM,
            pl.BlockSpec(memory_space=pl.ANY),
            VMEM,
            pl.BlockSpec(memory_space=pl.ANY),
        ],
        out_specs=VMEM,
        scratch_shapes=[
            pltpu.VMEM((2 * heads, latent), F32),
            pltpu.VMEM((latent // 128, rows, 128), F32),
            pltpu.VMEM((rows, width), BF16),
            pltpu.VMEM(keys_t.shape, BF16),
            pltpu.SMEM((slots + 1,), jnp.int32),
            pltpu.SMEM((1,), jnp.int32),
            pltpu.SemaphoreType.DMA,
            pltpu.SemaphoreType.DMA((keys_t.shape[1] // BLOCK,)),
        ],
        compiler_params=pltpu.CompilerParams(vmem_limit_bytes=60 * 1024 * 1024),
        name="attend",
    )(lengths, counts, queries.reshape(rows, width), new_key, keys_t)


def values_kernel(latent_ref, up_ref, whole_ref, upper_ref, lower_ref, sorted_ref):
    head_v = up_ref.shape[2]
    both = jnp.concatenate([up_ref[0], up_ref[1]], axis=1)
    mapped = jnp.dot(latent_ref[...], both, preferred_element_type=F32)
    for y in range(Y_SIZE):
        for z in range(Z_SIZE):
            source, target = 16 * (y * Z_SIZE + z), 8 * (z * Y_SIZE + y)
            sorted_ref[target : target + 8, :head_v] = mapped[source : source + 8, :head_v]
            sorted_ref[target : target + 8, head_v:] = mapped[source + 8 : source + 16, head_v:]
    whole = sorted_ref[...].astype(BF16)
    half = whole.shape[0] // 2
    whole_ref[...] = whole
    upper_ref[...] = whole[:half]
    lower_ref[...] = whole[half:]


def value_rows(latent_rows, value_up):
    return pl.pallas_call(
        values_kernel,
        out_shape=[jax.ShapeDtypeStruct((rows, 256), BF16) for rows in (256, 128, 128)],
        in_specs=[VMEM] * 2,
        out_specs=[VMEM] * 3,
        scratch_shapes=[pltpu.VMEM((256, 256), F32)],
        compiler_params=PARAMS,
        name="values",
    )(latent_rows, value_up)


def project_kernel(place_ref, *refs):
    values, weights = refs[:5], refs[5:10]
    out_ref, residual_ref, total_ref = refs[10:]
    weight = [ref[...] for ref in weights]
    parts = [weight[0][:256], weight[1][:256], None, weight[4][:256]]
    parts[2] = jnp.concatenate([weight[2][:128], weight[3]], axis=0)
    rows = [values[0][...], values[1][...], None, values[4][...]]
    rows[2] = jnp.concatenate([values[2][...], values[3][...]], axis=0)
    total_ref[...] = jnp.dot(rows[0], parts[0], preferred_element_type=F32)
    for k in (1, 2, 3):
        total_ref[...] += jnp.dot(rows[k], parts[k], preferred_element_type=F32)
    out_ref[...] = total_ref[...].astype(BF16)
    tails = [weight[0][256:], weight[1][256:], weight[2][128:], weight[4][256:]]
    for k in range(Y_SIZE):
        tail = tails[k].astype(F32)
        first = pl.multiple_of(lax.rem(place_ref[0] + Y_SIZE - k, Y_SIZE) * 8, 8)
        residual_ref[pl.ds(first, 8), :] = tail[:8] + tail[8:]


def project(place, values, weights):
    width = weights[0].shape[1]
    return pl.pallas_call(
        project_kernel,
        out_shape=[
            jax.ShapeDtypeStruct((256, width), BF16),
            jax.ShapeDtypeStruct((8 * Y_SIZE, width), F32),
        ],
        in_specs=[SMEM] + [VMEM] * 10,
        out_specs=[VMEM] * 2,
        scratch_shapes=[pltpu.VMEM((256, width), F32)],
        compiler_params=PARAMS,
        name="project",
    )(place, *values, *weights)


def feed_kernel(place_ref, *refs):
    quarters, gain_ref, gate_refs, down_ref = refs[:5], refs[5], refs[6:8], refs[8]
    outs, own_ref = refs[9:14], refs[14]
    state_ref, normed_ref, hidden_ref, turned_ref = refs[15:]
    _, _, hidden_width, depth = gate_refs[0].shape
    width = down_ref.shape[1]
    quarter_width = width // Y_SIZE
    my_y, chip, core, my_z = place_ref[0], place_ref[1], place_ref[2], place_ref[3]
    state_ref[0] = quarters[0][...].astype(F32)
    state_ref[1] = quarters[1][...].astype(F32)
    state_ref[2, :128] = quarters[2][...].astype(F32)
    state_ref[2, 128:] = quarters[3][...].astype(F32)
    state_ref[3] = quarters[4][...].astype(F32)
    square_sum = jnp.zeros((256, 1), F32)
    for k in range(Y_SIZE):
        square_sum += jnp.sum(state_ref[k] * state_ref[k], axis=1, keepdims=True)
    scale = lax.rsqrt(square_sum / width + NORM_EPS)
    own_first = pl.multiple_of((my_z * Y_SIZE + my_y) * 8, 8)
    for k in range(Y_SIZE):
        quarter = lax.rem(my_y + Y_SIZE - k, Y_SIZE)
        column = pl.multiple_of(quarter * quarter_width, quarter_width)
        own_ref[:, pl.ds(column, quarter_width)] = state_ref[k, pl.ds(own_first, 8), :]
        normed = (state_ref[k] * scale * gain_ref[quarter].astype(F32)).astype(BF16)
        normed_ref[2 * quarter] = normed[:, :depth]
        normed_ref[2 * quarter + 1] = normed[:, depth:]
    contract = (((1,), (1,)), ((), ()))
    gate = jnp.zeros((256, hidden_width), F32)
    upward = jnp.zeros((256, hidden_width), F32)
    for k in range(X_SIZE):
        for other in range(2):
            source = 2 * lax.rem(chip + X_SIZE - k, X_SIZE) + lax.rem(core + other, 2)
            piece = normed_ref[source]
            gate += lax.dot_general(
                piece, gate_refs[other][k, 0], contract, preferred_element_type=F32
            )
            upward += lax.dot_general(
                piece, gate_refs[other][k, 1], contract, preferred_element_type=F32
            )
    hidden = gate / (1.0 + jnp.exp(-gate)) * upward
    for z in range(Z_SIZE):
        for y in range(Y_SIZE):
            first = 8 * (z * Y_SIZE + y)
            hidden_ref[y, 8 * z : 8 * z + 8, :] = hidden[first : first + 8]
    for k in range(Y_SIZE):
        target = lax.rem(my_y + Y_SIZE - k, Y_SIZE)
        turned_ref[64 * k : 64 * k + 64, :] = hidden_ref[target].astype(BF16)
    for c in range(0, width, 512):
        part = jnp.dot(
            turned_ref[...], down_ref[:, c : c + 512], preferred_element_type=F32
        ).astype(BF16)
        store_blocks(outs, part, c)


def feed(place, quarters, gain, gate_pieces, down_proj):
    width = down_proj.shape[1]
    depth = gate_pieces[0].shape[-1]
    hidden_width = down_proj.shape[0]
    return pl.pallas_call(
        feed_kernel,
        out_shape=block_shapes(width) + [jax.ShapeDtypeStruct((8, width), F32)],
        in_specs=[SMEM] + [VMEM] * 9,
        out_specs=[VMEM] * 6,
        scratch_shapes=[
            pltpu.VMEM((Y_SIZE, 256, width // Y_SIZE), F32),
            pltpu.VMEM((width // depth, 256, depth), BF16),
            pltpu.VMEM((Y_SIZE, 64, hidden_width), F32),
            pltpu.VMEM((256, hidden_width), BF16),
        ],
        compiler_params=PARAMS,
        name="feed",
    )(place, *quarters, gain, *gate_pieces, down_proj)


def sum_over_y(blocks, direction):
    far = [y_shift(half, 2) for half in blocks[2]]
    near = [y_shift(blocks[k], direction * k) for k in (1, 3)]
    arrived = [blocks[0], jnp.concatenate(far, axis=0)] + near
    return sum(block.astype(F32) for block in arrived).astype(BF16)


def sum_over_z(column):
    rows, width = column.shape
    pieces = z_exchange(column).reshape(Z_SIZE, rows // Z_SIZE, width)
    return jnp.sum(pieces.astype(F32), axis=0)


def weight_shares(my_y, output_proj, residual):
    width = output_proj.shape[1] // Y_SIZE
    high = lax.reduce_precision(residual, exponent_bits=8, mantissa_bits=7)
    low = (residual - high).astype(BF16)
    high = high.astype(BF16)
    shares = []
    for k in range(Y_SIZE):
        column = ((my_y + k) % Y_SIZE) * width
        share = [
            lax.dynamic_slice_in_dim(part, column, width, 1) for part in (output_proj, high, low)
        ]
        if k == 2:
            half = share[0].shape[0] // 2
            shares.append(jnp.concatenate([share[0][:half], share[1], share[2]], axis=0))
            shares.append(share[0][half:])
        else:
            shares.append(jnp.concatenate(share, axis=0))
    return shares


def local(
    queries,
    new_key,
    latent_cache,
    lengths,
    counts,
    residual,
    value_up,
    output_proj,
    norm_gain,
    gate_up,
    down_proj,
):
    slots, heads, _ = queries.shape
    latent = value_up.shape[1]
    width = output_proj.shape[1]
    rank, group = lax.axis_index("tp"), lax.axis_index("dp")
    my_y = rank // Z_SIZE
    place = jnp.stack([my_y, group // 2, group % 2, rank % Z_SIZE]).astype(jnp.int32)
    gate_own = gate_up.transpose(0, 2, 1)
    gate_pieces = [gate_own] + [dp_shift(gate_own, k, 0) for k in (1, 2, 3)]

    latent_out = attend(lengths, counts, queries, new_key, latent_cache.T, latent)
    latent_out, output_proj, residual = lax.optimization_barrier(
        (latent_out, output_proj, residual)
    )
    outgoing = latent_out.reshape(32, 2 * slots, latent)
    shares = weight_shares(my_y, output_proj, residual)
    steps = (0, 1, 2, 2, 3)
    weights = [shares[0]] + [y_shift(share, k) for share, k in zip(shares[1:], steps[1:])]
    incoming = lax.all_to_all(outgoing, "tp", split_axis=0, concat_axis=0, tiled=True)
    incoming, gate_pieces[1], gate_pieces[3], *weights = lax.optimization_barrier(
        (incoming, gate_pieces[1], gate_pieces[3], *weights)
    )

    whole, upper, lower = value_rows(incoming.reshape(heads * slots, latent), value_up)
    values = [whole, y_shift(whole, 1), y_shift(upper, 2), y_shift(lower, 2), y_shift(whole, 3)]
    partial, residual_part = project(place, values, weights)
    state = sum_over_z(partial) + residual_part
    state, gate_pieces[2] = lax.optimization_barrier((state.astype(BF16), gate_pieces[2]))
    gate_mine = jnp.stack(gate_pieces)
    gate_mine = [gate_mine, dp_shift(gate_mine, 0, 1)]

    quarter = z_exchange(jnp.tile(state, (Z_SIZE, 1)))
    quarters = [
        quarter,
        y_shift(quarter, 1),
        y_shift(quarter[:128], 2),
        y_shift(quarter[128:], 2),
        y_shift(quarter, 3),
    ]
    gain = norm_gain.reshape(Y_SIZE, 1, width // Y_SIZE)
    *terms, own_state = feed(place, quarters, gain, gate_mine, down_proj)
    mixed = sum_over_z(sum_over_y(grouped(terms), -1)) + own_state
    live_mask = jnp.arange(slots, dtype=jnp.int32) < counts[0]
    return jnp.where(live_mask[:, None], mixed, 0.0).astype(BF16)


def solution(mesh):
    placed = (
        P(("dp", "tp"), None, None),
        P(("dp", "tp"), None),
        P(("dp", "tp"), None),
        P(("dp", "tp")),
        P(("dp", "tp")),
        P(("dp", "tp"), None),
        P("tp", None, None),
        P("tp", None),
        P(),
        P(None, "dp", "tp"),
        P("tp", None),
    )
    return jax.shard_map(
        local, mesh=mesh, in_specs=placed, out_specs=P(("dp", "tp"), None), check_vma=False
    )
```

```python
import functools

import jax
import jax.numpy as jnp
from jax import lax
from jax.experimental import pallas as pl
from jax.experimental.pallas import tpu as pltpu
from jax.sharding import PartitionSpec as P

SOFTMAX_SCALE = 192.0 ** (-0.5)
NORM_EPS = 1e-06
X_SIZE = 4
Y_SIZE = 4
Z_SIZE = 8
BLOCK = 512
RING_STATE, RING_GATHER, RING_DOWN = True, False, False
Z_GROUPS = [[y * Z_SIZE + z for z in range(Z_SIZE)] for y in range(Y_SIZE)]
BF16 = jnp.bfloat16
F32 = jnp.float32
VMEM = pl.BlockSpec(memory_space=pltpu.VMEM)
SMEM = pl.BlockSpec(memory_space=pltpu.SMEM)
PARAMS = pltpu.CompilerParams(vmem_limit_bytes=40 * 1024 * 1024)


def y_shift(array, step):
    pairs = [
        (y * Z_SIZE + z, ((y + step) % Y_SIZE) * Z_SIZE + z)
        for y in range(Y_SIZE)
        for z in range(Z_SIZE)
    ]
    return lax.ppermute(array, "tp", pairs)


def z_exchange(array):
    return lax.all_to_all(
        array, "tp", split_axis=0, concat_axis=0, tiled=True, axis_index_groups=Z_GROUPS
    )


def block_shapes(width):
    return [jax.ShapeDtypeStruct((rows, width), BF16) for rows in (64, 64, 32, 32, 64)]


def store_blocks(outs, part, column):
    for out, first in zip(outs, (0, 64, 128, 160, 192)):
        rows = out.shape[0]
        out[:, column : column + part.shape[1]] = part[first : first + rows]


def grouped(blocks):
    return [blocks[0], blocks[1], (blocks[2], blocks[3]), blocks[4]]


def dp_shift(array, turn, swap):
    pairs = [
        (2 * x + core, 2 * ((x + turn) % X_SIZE) + (core + swap) % 2)
        for x in range(X_SIZE)
        for core in range(2)
    ]
    return lax.ppermute(array, "dp", pairs)


def attend_kernel(
    lengths_ref,
    counts_ref,
    all_queries_ref,
    new_key_ref,
    cache_ref,
    out_ref,
    acc_ref,
    turned_ref,
    query_ref,
    keys_ref,
    bounds_ref,
    seen_ref,
    query_sem,
    sems,
):
    slots, heads = 8, 64
    latent = out_ref.shape[1]
    query_copy = pltpu.make_async_copy(all_queries_ref, query_ref, query_sem)
    query_copy.start()
    bounds_ref[0] = 0
    for s in range(slots):
        bounds_ref[s + 1] = bounds_ref[s] + jnp.where(s < counts_ref[0], lengths_ref[s], 0)
    blocks = (bounds_ref[slots] + BLOCK - 1) // BLOCK

    def arrival(block):
        span = pl.ds(pl.multiple_of(block * BLOCK, BLOCK), BLOCK)
        return pltpu.make_async_copy(cache_ref.at[:, span], keys_ref.at[:, span], sems.at[block])

    lax.fori_loop(0, blocks, lambda block, _: arrival(block).start(), None)
    seen_ref[0] = 0
    query_copy.wait()
    for pair in range(slots // 2):
        first = 2 * pair
        rows = pl.ds(first * heads, 2 * heads)
        query = query_ref[rows, :]
        own_rows = []
        for s in (first, first + 1):
            own_rows.append(
                jnp.broadcast_to(new_key_ref[s : s + 1, :].astype(F32), (heads, query.shape[1]))
            )
        own_keys = jnp.concatenate(own_rows, axis=0)
        own_score = (
            jnp.sum(query.astype(F32) * own_keys, axis=1, keepdims=True) * SOFTMAX_SCALE
        )
        acc_ref[...] = own_keys[:, :latent]
        is_second = lax.broadcasted_iota(jnp.int32, (2 * heads, 1), 0) >= heads
        row_start = jnp.where(is_second, bounds_ref[first + 1], bounds_ref[first])
        row_end = jnp.where(is_second, bounds_ref[first + 2], bounds_ref[first + 1])
        begin = bounds_ref[first] // BLOCK
        end = (bounds_ref[first + 2] + BLOCK - 1) // BLOCK
        end = jnp.where(bounds_ref[first + 2] > bounds_ref[first], end, begin)

        def step(block, carry):
            top, total = carry

            @pl.when(block == seen_ref[0])
            def _():
                arrival(block).wait()
                seen_ref[0] = block + 1

            offset = pl.multiple_of(block * BLOCK, BLOCK)
            scores = (
                jnp.dot(query, keys_ref[:, pl.ds(offset, BLOCK)], preferred_element_type=F32)
                * SOFTMAX_SCALE
            )
            positions = offset + lax.broadcasted_iota(jnp.int32, (1, BLOCK), 1)
            inside = (positions >= row_start) & (positions < row_end)
            scores = jnp.where(inside, scores, -1e30)
            new_top = jnp.maximum(top, jnp.max(scores, axis=1, keepdims=True))
            decay = jnp.exp(top - new_top)
            probs = jnp.exp(scores - new_top)
            new_total = total * decay + jnp.sum(probs, axis=1, keepdims=True)
            acc_ref[...] = acc_ref[...] * decay + lax.dot_general(
                probs.astype(BF16),
                keys_ref[:latent, pl.ds(offset, BLOCK)],
                (((1,), (1,)), ((), ())),
                preferred_element_type=F32,
            )
            return new_top, new_total

        _, total = lax.fori_loop(begin, end, step, (own_score, jnp.ones_like(own_score)))
        result = acc_ref[...] / total
        for s in (0, 1):
            for c in range(latent // 128):
                turned_ref[c, pl.ds(first + s, heads, slots), :] = result[
                    s * heads : (s + 1) * heads, 128 * c : 128 * c + 128
                ]
    for c in range(latent // 128):
        out_ref[:, 128 * c : 128 * c + 128] = turned_ref[c].astype(BF16)


def attend(lengths, counts, queries, new_key, keys_t, latent):
    slots, heads, width = queries.shape
    rows = slots * heads
    return pl.pallas_call(
        attend_kernel,
        out_shape=jax.ShapeDtypeStruct((rows, latent), BF16),
        in_specs=[
            SMEM,
            SMEM,
            pl.BlockSpec(memory_space=pl.ANY),
            VMEM,
            pl.BlockSpec(memory_space=pl.ANY),
        ],
        out_specs=VMEM,
        scratch_shapes=[
            pltpu.VMEM((2 * heads, latent), F32),
            pltpu.VMEM((latent // 128, rows, 128), F32),
            pltpu.VMEM((rows, width), BF16),
            pltpu.VMEM(keys_t.shape, BF16),
            pltpu.SMEM((slots + 1,), jnp.int32),
            pltpu.SMEM((1,), jnp.int32),
            pltpu.SemaphoreType.DMA,
            pltpu.SemaphoreType.DMA((keys_t.shape[1] // BLOCK,)),
        ],
        compiler_params=pltpu.CompilerParams(vmem_limit_bytes=60 * 1024 * 1024),
        name="attend",
    )(lengths, counts, queries.reshape(rows, width), new_key, keys_t)


def project_kernel(y_ref, latent_ref, up_ref, proj_ref, *refs):
    outs, values_ref, turned_ref = refs[:5], refs[5], refs[6]
    head_v = up_ref.shape[2]
    both = jnp.concatenate([up_ref[0], up_ref[1]], axis=1)
    mapped = jnp.dot(latent_ref[...], both, preferred_element_type=F32)
    mapped = mapped.reshape(32, 2, 8, 2 * head_v)
    values_ref[...] = jnp.concatenate(
        [
            mapped[:, 0, :, :head_v].reshape(256, head_v),
            mapped[:, 1, :, head_v:].reshape(256, head_v),
        ],
        axis=1,
    ).astype(BF16)
    for k in range(Y_SIZE):
        source = pl.multiple_of(lax.rem(y_ref[0] + k, Y_SIZE) * 64, 64)
        turned_ref[64 * k : 64 * k + 64, :] = values_ref[pl.ds(source, 64), :]
    width = proj_ref.shape[1]
    for c in range(0, width, 512):
        part = jnp.dot(
            turned_ref[...], proj_ref[:, c : c + 512], preferred_element_type=F32
        ).astype(BF16)
        store_blocks(outs, part, c)


def project(my_y, latent_rows, value_up, output_proj):
    width = output_proj.shape[1]
    return pl.pallas_call(
        project_kernel,
        out_shape=block_shapes(width),
        in_specs=[SMEM, VMEM, VMEM, VMEM],
        out_specs=[VMEM] * 5,
        scratch_shapes=[pltpu.VMEM((256, 256), BF16), pltpu.VMEM((256, 256), BF16)],
        compiler_params=PARAMS,
        name="project",
    )(my_y, latent_rows, value_up, output_proj)


def feed_kernel(place_ref, *refs):
    rows_refs, gate_refs, down_ref = refs[:5], refs[5:7], refs[7]
    outs, normed_ref, hidden_ref = refs[8:13], refs[13], refs[14]
    _, _, hidden_width, depth = gate_refs[0].shape
    parts = normed_ref.shape[0]
    for rows, first in zip(rows_refs, (0, 64, 128, 160, 192)):
        block = rows[...]
        for d in range(parts):
            normed_ref[d, first : first + rows.shape[0], :] = block[:, d * depth : (d + 1) * depth]
    contract = (((1,), (1,)), ((), ()))
    gate = jnp.zeros((256, hidden_width), F32)
    upward = jnp.zeros((256, hidden_width), F32)
    for k in range(X_SIZE):
        for other in range(2):
            chip = lax.rem(place_ref[1] + X_SIZE - k, X_SIZE)
            core = lax.rem(place_ref[2] + other, 2)
            piece = normed_ref[2 * chip + core]
            gate += lax.dot_general(
                piece, gate_refs[other][k, 0], contract, preferred_element_type=F32
            )
            upward += lax.dot_general(
                piece, gate_refs[other][k, 1], contract, preferred_element_type=F32
            )
    hidden_ref[...] = (gate / (1.0 + jnp.exp(-gate)) * upward).astype(BF16)
    width = down_ref.shape[1]
    for c in range(0, width, 512):
        part = jnp.dot(
            hidden_ref[...], down_ref[:, c : c + 512], preferred_element_type=F32
        ).astype(BF16)
        store_blocks(outs, part, c)


def feed(place, row_blocks, gate_pieces, down_proj):
    width = down_proj.shape[1]
    depth = gate_pieces[0].shape[-1]
    return pl.pallas_call(
        feed_kernel,
        out_shape=block_shapes(width),
        in_specs=[SMEM] + [VMEM] * 8,
        out_specs=[VMEM] * 5,
        scratch_shapes=[
            pltpu.VMEM((width // depth, 256, depth), BF16),
            pltpu.VMEM((256, down_proj.shape[0]), BF16),
        ],
        compiler_params=PARAMS,
        name="feed",
    )(place, *row_blocks, *gate_pieces, down_proj)


def sum_over_y(blocks, direction, ring):
    if ring:
        upper = y_shift(blocks[2][0], direction)
        lower = y_shift(blocks[2][1], -direction)
        half = upper.shape[0]
        ahead = blocks[1].astype(F32) + jnp.pad(upper.astype(F32), ((0, half), (0, 0)))
        behind = blocks[3].astype(F32) + jnp.pad(lower.astype(F32), ((half, 0), (0, 0)))
        arrived = [
            blocks[0],
            y_shift(ahead.astype(BF16), direction),
            y_shift(behind.astype(BF16), -direction),
        ]
    else:
        far = [y_shift(part, 2) for part in blocks[2]]
        near = [y_shift(blocks[k], direction * k) for k in (1, 3)]
        arrived = [blocks[0], jnp.concatenate(far, axis=0)] + near
    return sum(block.astype(F32) for block in arrived).astype(BF16)


def gather_over_y(column, ring):
    half = column.shape[0] // 2
    one, three = y_shift(column, 1), y_shift(column, 3)
    if ring:
        far = [y_shift(one[:half], 1), y_shift(three[half:], 3)]
    else:
        far = [y_shift(column[:half], 2), y_shift(column[half:], 2)]
    return [column, one, *far, three]


def sum_over_z(column):
    pieces = z_exchange(column).reshape(Z_SIZE, 8, column.shape[1])
    return jnp.sum(pieces.astype(F32), axis=0)


def local(
    queries,
    new_key,
    latent_cache,
    lengths,
    counts,
    residual,
    value_up,
    output_proj,
    norm_gain,
    gate_up,
    down_proj,
):
    slots, heads, _ = queries.shape
    latent = value_up.shape[1]
    rank, group = lax.axis_index("tp"), lax.axis_index("dp")
    place = jnp.stack([rank // Z_SIZE, group // 2, group % 2]).astype(jnp.int32)

    latent_out = attend(lengths, counts, queries, new_key, latent_cache.T, latent)
    outgoing = latent_out.reshape(32, 2 * slots, latent)
    incoming = lax.all_to_all(outgoing, "tp", split_axis=0, concat_axis=0, tiled=True)
    gate_own = gate_up.transpose(0, 2, 1)
    gate_pieces = [gate_own, dp_shift(gate_own, 1, 0), None, dp_shift(gate_own, 3, 0)]
    incoming, gate_pieces[1], gate_pieces[3] = lax.optimization_barrier(
        (incoming, gate_pieces[1], gate_pieces[3])
    )
    gate_pieces[2] = jnp.stack([dp_shift(gate_pieces[1][0], 1, 0), dp_shift(gate_pieces[3][1], 3, 0)])

    terms = project(place, incoming.reshape(64 * slots, latent), value_up, output_proj)
    column = sum_over_y(grouped(terms), 1, RING_STATE)
    column, gate_pieces[2] = lax.optimization_barrier((column, gate_pieces[2]))
    gate_mine = jnp.stack(gate_pieces)
    gate_mine = [gate_mine, dp_shift(gate_mine, 0, 1)]
    state = sum_over_z(column) + residual
    mean_square = jnp.mean(state * state, axis=-1, keepdims=True)
    normed = (state * lax.rsqrt(mean_square + NORM_EPS) * norm_gain.astype(F32)).astype(BF16)

    column = z_exchange(jnp.tile(normed, (Z_SIZE, 1)))
    blocks = gather_over_y(column, RING_GATHER)
    terms = feed(place, blocks, gate_mine, down_proj)
    mixed = sum_over_z(sum_over_y(grouped(terms), -1, RING_DOWN)) + state
    live_mask = jnp.arange(slots, dtype=jnp.int32) < counts[0]
    return jnp.where(live_mask[:, None], mixed, 0.0).astype(BF16)


def solution(mesh):
    placed = (
        P(("dp", "tp"), None, None),
        P(("dp", "tp"), None),
        P(("dp", "tp"), None),
        P(("dp", "tp")),
        P(("dp", "tp")),
        P(("dp", "tp"), None),
        P("tp", None, None),
        P("tp", None),
        P(),
        P(None, "dp", "tp"),
        P("tp", None),
    )
    return jax.shard_map(
        local, mesh=mesh, in_specs=placed, out_specs=P(("dp", "tp"), None), check_vma=False
    )
```

```python
import functools

import jax
import jax.numpy as jnp
from jax import lax
from jax.experimental import pallas as pl
from jax.experimental.pallas import tpu as pltpu
from jax.sharding import PartitionSpec as P

SOFTMAX_SCALE = 192.0 ** (-0.5)
NORM_EPS = 1e-06
X_SIZE = 4
Y_SIZE = 4
Z_SIZE = 8
BLOCK = 512
RING_STATE, RING_GATHER, RING_DOWN = True, False, False
Z_GROUPS = [[y * Z_SIZE + z for z in range(Z_SIZE)] for y in range(Y_SIZE)]
BF16 = jnp.bfloat16
F32 = jnp.float32
VMEM = pl.BlockSpec(memory_space=pltpu.VMEM)
SMEM = pl.BlockSpec(memory_space=pltpu.SMEM)
PARAMS = pltpu.CompilerParams(vmem_limit_bytes=40 * 1024 * 1024)


def y_shift(array, step):
    pairs = [
        (y * Z_SIZE + z, ((y + step) % Y_SIZE) * Z_SIZE + z)
        for y in range(Y_SIZE)
        for z in range(Z_SIZE)
    ]
    return lax.ppermute(array, "tp", pairs)


def z_exchange(array):
    return lax.all_to_all(
        array, "tp", split_axis=0, concat_axis=0, tiled=True, axis_index_groups=Z_GROUPS
    )


def block_shapes(width):
    return [jax.ShapeDtypeStruct((rows, width), BF16) for rows in (64, 64, 32, 32, 64)]


def store_blocks(outs, part, column):
    for out, first in zip(outs, (0, 64, 128, 160, 192)):
        rows = out.shape[0]
        out[:, column : column + part.shape[1]] = part[first : first + rows]


def grouped(blocks):
    return [blocks[0], blocks[1], (blocks[2], blocks[3]), blocks[4]]


def dp_shift(array, turn, swap):
    pairs = [
        (2 * x + core, 2 * ((x + turn) % X_SIZE) + (core + swap) % 2)
        for x in range(X_SIZE)
        for core in range(2)
    ]
    return lax.ppermute(array, "dp", pairs)


def attend_kernel(
    lengths_ref,
    counts_ref,
    all_queries_ref,
    new_key_ref,
    cache_ref,
    out_ref,
    acc_ref,
    top_ref,
    total_ref,
    even_ref,
    odd_ref,
    turned_ref,
    query_ref,
    keys_ref,
    bounds_ref,
    pair_ref,
    block_ref,
    seen_ref,
    query_sem,
    sems,
):
    slots, heads = 8, 64
    pairs = slots // 2
    latent = out_ref.shape[1]
    query_copy = pltpu.make_async_copy(all_queries_ref, query_ref, query_sem)
    query_copy.start()
    bounds_ref[0] = 0
    for s in range(slots):
        bounds_ref[s + 1] = bounds_ref[s] + jnp.where(s < counts_ref[0], lengths_ref[s], 0)
    blocks = (bounds_ref[slots] + BLOCK - 1) // BLOCK

    def arrival(block):
        span = pl.ds(pl.multiple_of(block * BLOCK, BLOCK), BLOCK)
        return pltpu.make_async_copy(cache_ref.at[:, span], keys_ref.at[:, span], sems.at[block])

    lax.fori_loop(0, blocks, lambda block, _: arrival(block).start(), None)
    seen_ref[0] = 0

    items = 0
    for pair in range(pairs):
        low, high = bounds_ref[2 * pair], bounds_ref[2 * pair + 2]
        begin = low // BLOCK
        end = jnp.where(high > low, (high + BLOCK - 1) // BLOCK, begin)

        def note(block, item, pair=pair):
            pair_ref[item] = pair
            block_ref[item] = block
            return item + 1

        items = lax.fori_loop(begin, end, note, items)
    for extra in range(3):
        pair_ref[items + extra] = pairs
        block_ref[items + extra] = 0

    query_copy.wait()
    for pair in range(pairs):
        query = query_ref[pl.ds(2 * pair * heads, 2 * heads), :]
        own_rows = []
        for s in (2 * pair, 2 * pair + 1):
            own_rows.append(
                jnp.broadcast_to(new_key_ref[s : s + 1, :].astype(F32), (heads, query.shape[1]))
            )
        own_keys = jnp.concatenate(own_rows, axis=0)
        top_ref[pair] = (
            jnp.sum(query.astype(F32) * own_keys, axis=1, keepdims=True) * SOFTMAX_SCALE
        )
        total_ref[pair] = jnp.ones((2 * heads, 1), F32)
        acc_ref[pair] = own_keys[:, :latent]
    is_second = lax.broadcasted_iota(jnp.int32, (2 * heads, 1), 0) >= heads

    def fetch(item):
        block = block_ref[item]

        @pl.when((block == seen_ref[0]) & (block < blocks))
        def _():
            arrival(block).wait()
            seen_ref[0] = block + 1

    def score(item, score_ref):
        pair = jnp.minimum(pair_ref[item], pairs - 1)
        offset = pl.multiple_of(block_ref[item] * BLOCK, BLOCK)
        rows = pl.ds(pl.multiple_of(pair * 2 * heads, 2 * heads), 2 * heads)
        score_ref[...] = jnp.dot(
            query_ref[rows, :], keys_ref[:, pl.ds(offset, BLOCK)], preferred_element_type=F32
        )

    def absorb(item, score_ref):
        filler = pair_ref[item] == pairs
        pair = jnp.minimum(pair_ref[item], pairs - 1)
        offset = pl.multiple_of(block_ref[item] * BLOCK, BLOCK)
        low, middle, high = (bounds_ref[2 * pair + s] for s in range(3))
        row_start = jnp.where(is_second, middle, low)
        row_end = jnp.where(is_second, high, middle)
        row_end = jnp.where(filler, row_start, row_end)
        positions = offset + lax.broadcasted_iota(jnp.int32, (1, BLOCK), 1)
        inside = (positions >= row_start) & (positions < row_end)
        scores = jnp.where(inside, score_ref[...] * SOFTMAX_SCALE, -1e30)
        top = top_ref[pair]
        new_top = jnp.maximum(top, jnp.max(scores, axis=1, keepdims=True))
        decay = jnp.exp(top - new_top)
        probs = jnp.exp(scores - new_top)
        top_ref[pair] = new_top
        total_ref[pair] = total_ref[pair] * decay + jnp.sum(probs, axis=1, keepdims=True)
        acc_ref[pair] = acc_ref[pair] * decay + lax.dot_general(
            probs.astype(BF16),
            keys_ref[:latent, pl.ds(offset, BLOCK)],
            (((1,), (1,)), ((), ())),
            preferred_element_type=F32,
        )

    @pl.when(items > 0)
    def _():
        fetch(0)
        score(0, even_ref)

        def step(j, _):
            fetch(2 * j + 1)
            fetch(2 * j + 2)
            score(2 * j + 1, odd_ref)
            absorb(2 * j, even_ref)
            score(2 * j + 2, even_ref)
            absorb(2 * j + 1, odd_ref)

        lax.fori_loop(0, (items + 1) // 2, step, None)

    for pair in range(pairs):
        result = acc_ref[pair] / total_ref[pair]
        for s in (0, 1):
            for c in range(latent // 128):
                turned_ref[c, pl.ds(2 * pair + s, heads, slots), :] = result[
                    s * heads : (s + 1) * heads, 128 * c : 128 * c + 128
                ]
    for c in range(latent // 128):
        out_ref[:, 128 * c : 128 * c + 128] = turned_ref[c].astype(BF16)


def attend(lengths, counts, queries, new_key, keys_t, latent):
    slots, heads, width = queries.shape
    rows = slots * heads
    return pl.pallas_call(
        attend_kernel,
        out_shape=jax.ShapeDtypeStruct((rows, latent), BF16),
        in_specs=[
            SMEM,
            SMEM,
            pl.BlockSpec(memory_space=pl.ANY),
            VMEM,
            pl.BlockSpec(memory_space=pl.ANY),
        ],
        out_specs=VMEM,
        scratch_shapes=[
            pltpu.VMEM((slots // 2, 2 * heads, latent), F32),
            pltpu.VMEM((slots // 2, 2 * heads, 1), F32),
            pltpu.VMEM((slots // 2, 2 * heads, 1), F32),
            pltpu.VMEM((2 * heads, BLOCK), F32),
            pltpu.VMEM((2 * heads, BLOCK), F32),
            pltpu.VMEM((latent // 128, rows, 128), F32),
            pltpu.VMEM((rows, width), BF16),
            pltpu.VMEM(keys_t.shape, BF16),
            pltpu.SMEM((slots + 1,), jnp.int32),
            pltpu.SMEM((keys_t.shape[1] // BLOCK + slots + 3,), jnp.int32),
            pltpu.SMEM((keys_t.shape[1] // BLOCK + slots + 3,), jnp.int32),
            pltpu.SMEM((1,), jnp.int32),
            pltpu.SemaphoreType.DMA,
            pltpu.SemaphoreType.DMA((keys_t.shape[1] // BLOCK,)),
        ],
        compiler_params=pltpu.CompilerParams(vmem_limit_bytes=60 * 1024 * 1024),
        name="attend",
    )(lengths, counts, queries.reshape(rows, width), new_key, keys_t)


def project_kernel(y_ref, latent_ref, up_ref, proj_ref, *refs):
    outs, values_ref, turned_ref = refs[:5], refs[5], refs[6]
    head_v = up_ref.shape[2]
    both = jnp.concatenate([up_ref[0], up_ref[1]], axis=1)
    mapped = jnp.dot(latent_ref[...], both, preferred_element_type=F32)
    mapped = mapped.reshape(32, 2, 8, 2 * head_v)
    values_ref[...] = jnp.concatenate(
        [
            mapped[:, 0, :, :head_v].reshape(256, head_v),
            mapped[:, 1, :, head_v:].reshape(256, head_v),
        ],
        axis=1,
    ).astype(BF16)
    for k in range(Y_SIZE):
        source = pl.multiple_of(lax.rem(y_ref[0] + k, Y_SIZE) * 64, 64)
        turned_ref[64 * k : 64 * k + 64, :] = values_ref[pl.ds(source, 64), :]
    width = proj_ref.shape[1]
    for c in range(0, width, 512):
        part = jnp.dot(
            turned_ref[...], proj_ref[:, c : c + 512], preferred_element_type=F32
        ).astype(BF16)
        store_blocks(outs, part, c)


def project(my_y, latent_rows, value_up, output_proj):
    width = output_proj.shape[1]
    return pl.pallas_call(
        project_kernel,
        out_shape=block_shapes(width),
        in_specs=[SMEM, VMEM, VMEM, VMEM],
        out_specs=[VMEM] * 5,
        scratch_shapes=[pltpu.VMEM((256, 256), BF16), pltpu.VMEM((256, 256), BF16)],
        compiler_params=PARAMS,
        name="project",
    )(my_y, latent_rows, value_up, output_proj)


def feed_kernel(place_ref, *refs):
    rows_refs, gate_refs, down_ref = refs[:5], refs[5:7], refs[7]
    outs, normed_ref, hidden_ref, shards_ref, sem = refs[8:13], *refs[13:]
    _, _, hidden_width, depth = gate_refs[0].shape
    other_copy = pltpu.make_async_copy(gate_refs[1], shards_ref, sem)
    other_copy.start()
    parts = normed_ref.shape[0]
    for rows, first in zip(rows_refs, (0, 64, 128, 160, 192)):
        block = rows[...]
        for d in range(parts):
            normed_ref[d, first : first + rows.shape[0], :] = block[:, d * depth : (d + 1) * depth]
    contract = (((1,), (1,)), ((), ()))
    gate = jnp.zeros((256, hidden_width), F32)
    upward = jnp.zeros((256, hidden_width), F32)
    for other, shards in enumerate((gate_refs[0], shards_ref)):
        if other:
            other_copy.wait()
        for k in range(X_SIZE):
            chip = lax.rem(place_ref[1] + X_SIZE - k, X_SIZE)
            core = lax.rem(place_ref[2] + other, 2)
            piece = normed_ref[2 * chip + core]
            gate += lax.dot_general(piece, shards[k, 0], contract, preferred_element_type=F32)
            upward += lax.dot_general(piece, shards[k, 1], contract, preferred_element_type=F32)
    hidden_ref[...] = (gate / (1.0 + jnp.exp(-gate)) * upward).astype(BF16)
    width = down_ref.shape[1]
    for c in range(0, width, 512):
        part = jnp.dot(
            hidden_ref[...], down_ref[:, c : c + 512], preferred_element_type=F32
        ).astype(BF16)
        store_blocks(outs, part, c)


def feed(place, row_blocks, gate_pieces, down_proj):
    width = down_proj.shape[1]
    depth = gate_pieces[0].shape[-1]
    return pl.pallas_call(
        feed_kernel,
        out_shape=block_shapes(width),
        in_specs=[SMEM] + [VMEM] * 6 + [pl.BlockSpec(memory_space=pl.ANY), VMEM],
        out_specs=[VMEM] * 5,
        scratch_shapes=[
            pltpu.VMEM((width // depth, 256, depth), BF16),
            pltpu.VMEM((256, down_proj.shape[0]), BF16),
            pltpu.VMEM(gate_pieces[1].shape, BF16),
            pltpu.SemaphoreType.DMA,
        ],
        compiler_params=PARAMS,
        name="feed",
    )(place, *row_blocks, *gate_pieces, down_proj)


def sum_over_y(blocks, direction, ring):
    if ring:
        upper = y_shift(blocks[2][0], direction)
        lower = y_shift(blocks[2][1], -direction)
        half = upper.shape[0]
        ahead = blocks[1].astype(F32) + jnp.pad(upper.astype(F32), ((0, half), (0, 0)))
        behind = blocks[3].astype(F32) + jnp.pad(lower.astype(F32), ((half, 0), (0, 0)))
        arrived = [
            blocks[0],
            y_shift(ahead.astype(BF16), direction),
            y_shift(behind.astype(BF16), -direction),
        ]
    else:
        far = [y_shift(part, 2) for part in blocks[2]]
        near = [y_shift(blocks[k], direction * k) for k in (1, 3)]
        arrived = [blocks[0], jnp.concatenate(far, axis=0)] + near
    return sum(block.astype(F32) for block in arrived).astype(BF16)


def gather_over_y(column, ring):
    half = column.shape[0] // 2
    one, three = y_shift(column, 1), y_shift(column, 3)
    if ring:
        far = [y_shift(one[:half], 1), y_shift(three[half:], 3)]
    else:
        far = [y_shift(column[:half], 2), y_shift(column[half:], 2)]
    return [column, one, *far, three]


def sum_over_z(column):
    pieces = z_exchange(column).reshape(Z_SIZE, 8, column.shape[1])
    return jnp.sum(pieces.astype(F32), axis=0)


def local(
    queries,
    new_key,
    latent_cache,
    lengths,
    counts,
    residual,
    value_up,
    output_proj,
    norm_gain,
    gate_up,
    down_proj,
):
    slots, heads, _ = queries.shape
    latent = value_up.shape[1]
    rank, group = lax.axis_index("tp"), lax.axis_index("dp")
    place = jnp.stack([rank // Z_SIZE, group // 2, group % 2]).astype(jnp.int32)

    latent_out = attend(lengths, counts, queries, new_key, latent_cache.T, latent)
    outgoing = latent_out.reshape(32, 2 * slots, latent)
    incoming = lax.all_to_all(outgoing, "tp", split_axis=0, concat_axis=0, tiled=True)
    gate_own = gate_up.transpose(0, 2, 1)
    gate_pieces = [gate_own, dp_shift(gate_own, 1, 0), None, dp_shift(gate_own, 3, 0)]
    incoming, gate_pieces[1], gate_pieces[3] = lax.optimization_barrier(
        (incoming, gate_pieces[1], gate_pieces[3])
    )
    gate_pieces[2] = jnp.stack([dp_shift(gate_pieces[1][0], 1, 0), dp_shift(gate_pieces[3][1], 3, 0)])

    terms = project(place, incoming.reshape(64 * slots, latent), value_up, output_proj)
    column = sum_over_y(grouped(terms), 1, RING_STATE)
    column, gate_pieces[2] = lax.optimization_barrier((column, gate_pieces[2]))
    gate_mine = jnp.stack(gate_pieces)
    gate_mine = [gate_mine, dp_shift(gate_mine, 0, 1)]
    state = sum_over_z(column) + residual
    mean_square = jnp.mean(state * state, axis=-1, keepdims=True)
    normed = (state * lax.rsqrt(mean_square + NORM_EPS) * norm_gain.astype(F32)).astype(BF16)

    column = z_exchange(jnp.tile(normed, (Z_SIZE, 1)))
    blocks = gather_over_y(column, RING_GATHER)
    terms = feed(place, blocks, gate_mine, down_proj)
    mixed = sum_over_z(sum_over_y(grouped(terms), -1, RING_DOWN)) + state
    live_mask = jnp.arange(slots, dtype=jnp.int32) < counts[0]
    return jnp.where(live_mask[:, None], mixed, 0.0).astype(BF16)


def solution(mesh):
    placed = (
        P(("dp", "tp"), None, None),
        P(("dp", "tp"), None),
        P(("dp", "tp"), None),
        P(("dp", "tp")),
        P(("dp", "tp")),
        P(("dp", "tp"), None),
        P("tp", None, None),
        P("tp", None),
        P(),
        P(None, "dp", "tp"),
        P("tp", None),
    )
    return jax.shard_map(
        local, mesh=mesh, in_specs=placed, out_specs=P(("dp", "tp"), None), check_vma=False
    )
```
